32 devices in a mesh: pair: 8 (over z, x), cores: 2 (over core), split: 2 (over y).
Axes of the slice: x: 2, y: 2, z: 4, core: 2. Of those that a mesh axis runs over, the one named last changes fastest.
Arguments:
- summand_cores: float32 [8, 2, 128, 16, 128], P('pair', 'cores', None, 'split'), may hold values from -0.088388348 to 0.088388348
- sketch_cores: bfloat16 [2, 128, 16, 128], P('cores', None, 'split'), may hold values from -0.5 to 0.5
Outputs:
- rounded_cores: float32 [8, 2, 128, 16, 128], P('pair', 'cores', None, 'split')
The draws below stay inside these ranges and needn't reach their ends.
All inputs are finite; a program needn't handle non-finite values.
Results may differ from the reference program's by a relative error of at most 0.00035.
Values sent between devices are 32-bit elements; how exact they have to be, the bound alone decides.
A program may use at most 64 MiB of HBM per device.

```python
import jax
import jax.numpy as jnp
from jax import lax

RANK = 128
MODE = 16
TRAIN_CORES = 2
SUMMANDS = 8


def draw_summand_cores(key, part):
    spread = (RANK * MODE) ** (-0.5)
    decay = jnp.exp(-jnp.linspace(0.0, 8.0, RANK, dtype=jnp.float32))
    shape = (SUMMANDS, TRAIN_CORES, RANK, MODE, RANK)
    base = jax.random.normal(key, shape, jnp.float32)
    base = jnp.clip(base, -4.0, 4.0)
    return (base * spread * decay).astype(jnp.float32)


def steps_of(key, dims, cuts, least, largest):
    def one(axis_at, parts):
        draws = jax.random.uniform(jax.random.fold_in(jax.random.fold_in(key, 6), axis_at), (parts,), jnp.float32, least / len(cuts), largest / len(cuts))
        return jnp.repeat(jnp.exp(draws), dims[axis_at] // parts).reshape((-1,) + (1,) * (len(dims) - axis_at - 1))

    gain = one(*cuts[0])
    for cut in cuts[1:]:
        gain = gain * one(*cut)
    return gain


def scatter_about(key, extent, scale, reach, shards=(), kind=jnp.bfloat16):
    entries = jax.random.normal(key, extent, jnp.float32) * scale
    if len(shards) > 0:
        entries = steps_of(key, extent, shards, -0.22, 0.18) * entries
    return jnp.clip(entries, min=-reach, max=reach).astype(kind)


def setup_inputs(seed: int = 0) -> dict:
    seeds = jax.random.split(jax.random.key(seed), 3)
    return {
        "summand_cores": draw_summand_cores(jax.random.fold_in(seeds[2], 71), 0),
        "sketch_cores": scatter_about(seeds[1], (TRAIN_CORES, RANK, MODE, RANK), RANK ** -0.5, 0.5, ((0, 2), (2, 2))),
    }


highest = lax.Precision.HIGHEST
shift_ratio = 0.01

def contract_sketch(own_core, sketch_in, sketch_core):
    inner = jnp.einsum('aib,bm->aim', own_core, sketch_in, precision=highest)
    return jnp.einsum('aim,lim->al', inner, sketch_core, precision=highest)

def sketch_chain(train, sketch_cores):
    identity = jnp.eye(RANK, dtype=jnp.float32)
    current = identity
    inputs = []
    for position in range(TRAIN_CORES - 1, -1, -1):
        inputs.append(current)
        current = contract_sketch(train[position], current, sketch_cores[position])
    return jnp.stack(inputs[::-1])

def compress(own_train, other_train, own_next, other_next):
    identity = jnp.eye(RANK, dtype=jnp.float32)
    carry = jnp.concatenate([identity, identity], axis=1)
    out_scale = (RANK * MODE) ** 0.5
    pieces = []
    for position in range(TRAIN_CORES):
        moved_own = jnp.einsum('la,aib->lib', carry[:, :RANK], own_train[position], precision=highest)
        moved_other = jnp.einsum('la,aib->lib', carry[:, RANK:], other_train[position], precision=highest)
        if position == TRAIN_CORES - 1:
            pieces.append((moved_own + moved_other) * out_scale)
        else:
            image = jnp.einsum('lib,bm->lim', moved_own, own_next[position], precision=highest)
            image = image + jnp.einsum('lib,bm->lim', moved_other, other_next[position], precision=highest)
            gram_local = jnp.einsum('lim,lin->mn', image, image, precision=highest)
            shifted = gram_local + shift_ratio * jnp.trace(gram_local) / RANK * identity
            factor_low = jnp.linalg.cholesky(shifted)
            inverse = lax.linalg.triangular_solve(factor_low, identity, left_side=True, lower=True)
            ortho = jnp.einsum('lim,nm->lin', image, inverse, precision=highest)
            cross_own = jnp.einsum('lin,lib->nb', ortho, moved_own, precision=highest)
            cross_other = jnp.einsum('lin,lib->nb', ortho, moved_other, precision=highest)
            carry = jnp.concatenate([cross_own, cross_other], axis=1)
            pieces.append(ortho * out_scale)
    return jnp.stack(pieces)

def reference(summand_cores, sketch_cores):
    sketch_full = sketch_cores.astype(jnp.float32)
    nexts = lax.map(lambda train: sketch_chain(train, sketch_full), summand_cores)
    stride = SUMMANDS // 4

    def one_sum(index):
        partner = ((index + stride) % SUMMANDS).astype(jnp.int32)
        return compress(summand_cores[index], summand_cores[partner], nexts[index], nexts[partner])
    return lax.map(one_sum, jnp.arange(SUMMANDS, dtype=jnp.int32))
```

```python
import functools

import jax
import jax.numpy as jnp
from jax import lax
from jax.experimental import pallas as pl
from jax.experimental.pallas import tpu as pltpu
from jax.sharding import PartitionSpec as P

SHIFT_RATIO = 0.01
CHUNKS = 4
PANEL = 4
MESH = pl.DeviceIdType.MESH


def dot(a, b, dims=((1,), (0,))):
    return lax.dot_general(
        a, b, (dims, ((), ())), precision=lax.Precision.HIGHEST, preferred_element_type=jnp.float32
    )


def lower_inverse(shifted, inv_ref):
    n = shifted.shape[0]
    lane = lax.broadcasted_iota(jnp.int32, (1, n), 1)
    state = shifted
    top = 0
    for start in range(0, n, PANEL):
        inside = (lane >= start) & (lane < start + PANEL)
        cols, rows = [], []
        for j in range(start, start + PANEL):
            cols.append(jnp.broadcast_to(state[:, j : j + 1], state.shape))
            row = state[j - top : j - top + 1, :]
            rows.append(jnp.where(inside, jnp.where(lane == j, 1.0, 0.0), row))
        scaled = []
        for k in range(PANEL):
            at = start + k - top
            pivot = cols[k][at : at + 1, :]
            recip = 1.0 / pivot
            scaled.append(rows[k] * recip)
            for m in range(k + 1, PANEL):
                factor = cols[m][at : at + 1, :] * recip
                cols[m] = cols[m] - cols[k] * factor
                rows[m] = rows[m] - rows[k] * factor
            root = lax.rsqrt(pivot)
            root = root * (1.5 - 0.5 * pivot * root * root)
            inv_ref[start + k : start + k + 1, :] = jnp.where(lane <= start + k, rows[k] * root, 0.0)
        new_top = (start + PANEL) // 8 * 8
        if start + PANEL < n:
            drop = new_top - top
            update = jnp.where(inside, 0.0, state[drop:, :])
            for k in range(PANEL):
                update = update - cols[k][drop:, :] * scaled[k]
            state, top = update, new_top


def kernel(
    n_pair, depth, n_split, stride, scale,
    c_ref, sk_ref, out_ref,
    c_own, c_oth, sk32, y_buf, s_part, s_in, g_part, g_in, x_part, x_in, inv, carry_out, carry_in,
    local_sem, c_send, c_recv, s_send, s_recv, g_send, g_recv, x_send, x_recv, k_send, k_recv, go_sem,
):
    q = lax.axis_index("pair")
    p = lax.axis_index("cores")
    y = lax.axis_index("split")
    rank, modes, _ = c_own.shape
    last = depth - 1
    before = lax.rem(q - stride + n_pair, n_pair)
    after = lax.rem(q + stride, n_pair)

    def mate(d):
        return lax.rem(y + d + n_split, n_split)

    local = pltpu.make_async_copy(c_ref, c_own, local_sem)
    local.start()

    barrier = pltpu.get_barrier_semaphore()

    def greet(*place):
        pl.semaphore_signal(barrier, inc=1, device_id=place, device_id_type=MESH)

    greet(after, p, y)

    @pl.when(p < last)
    def _():
        for d in range(n_split):
            greet(q, p + 1, mate(d))
            greet(after, p + 1, mate(d))
        for d in range(1, n_split):
            greet(q, p, mate(-d))

    @pl.when(p > 0)
    def _():
        greet(q, p - 1, y)

    @pl.when(p == 0)
    def _():
        pl.semaphore_wait(barrier, 1 + (n_split - 1) + 1)

    if depth > 2:
        @pl.when((p > 0) & (p < last))
        def _():
            pl.semaphore_wait(barrier, 1 + (n_split - 1) + 1 + 2 * n_split)

    @pl.when(p == last)
    def _():
        pl.semaphore_wait(barrier, 1 + 2 * n_split)

    part = rank // CHUNKS

    def core_copy(k):
        rows = pl.ds(k * part, part)
        return pltpu.make_async_remote_copy(
            src_ref=c_ref.at[rows], dst_ref=c_oth.at[rows], send_sem=c_send.at[k], recv_sem=c_recv.at[k],
            device_id=(before, p, y), device_id_type=MESH,
        )

    def sketch_copy(which, d):
        return pltpu.make_async_remote_copy(
            src_ref=s_part, dst_ref=s_in.at[which, d],
            send_sem=s_send.at[which, d], recv_sem=s_recv.at[which, d],
            device_id=(q if which == 0 else before, p - 1, mate(d)), device_id_type=MESH,
        )

    def gram_copy(d):
        return pltpu.make_async_remote_copy(
            src_ref=g_part, dst_ref=g_in.at[d - 1], send_sem=g_send.at[d - 1], recv_sem=g_recv.at[d - 1],
            device_id=(q, p, mate(d)), device_id_type=MESH,
        )

    def cross_copy(d):
        return pltpu.make_async_remote_copy(
            src_ref=x_part, dst_ref=x_in.at[d - 1], send_sem=x_send.at[d - 1], recv_sem=x_recv.at[d - 1],
            device_id=(q, p, mate(d)), device_id_type=MESH,
        )

    def carry_copy():
        return pltpu.make_async_remote_copy(
            src_ref=carry_out, dst_ref=carry_in, send_sem=k_send, recv_sem=k_recv,
            device_id=(q, p + 1, y), device_id_type=MESH,
        )

    def send_core():
        for k in range(CHUNKS):
            core_copy(k).start()

    def receive_sketch():
        for which in range(2):
            for d in range(n_split):
                sketch_copy(which, d).wait_recv()
            total = s_in[which, 0]
            for d in range(1, n_split):
                total = total + s_in[which, d]
            s_in[which, 0] = total

    def send_sketch(at_end):
        sk32[...] = sk_ref[...].astype(jnp.float32)
        local.wait()
        if at_end:
            left = jnp.concatenate([c_own[:, i, :] for i in range(modes)], axis=1)
        else:
            inner = dot(c_own[...].reshape(rank * modes, rank), s_in[0, 0])
            y_buf[...] = inner.reshape(rank, modes, rank)
            left = jnp.concatenate([y_buf[:, i, :] for i in range(modes)], axis=1)
        right = jnp.concatenate([sk32[:, i, :] for i in range(modes)], axis=1)
        s_part[...] = dot(left, right, ((1,), (1,)))
        for which in (1, 0):
            for d in range(n_split):
                sketch_copy(which, d).start()

    def finish_sketch():
        for which in range(2):
            for d in range(n_split):
                sketch_copy(which, d).wait_send()

    def compress(waits):
        own_in, oth_in = s_in[0, 0], s_in[1, 0]
        gram = jnp.zeros((rank, rank), jnp.float32)
        for k in range(CHUNKS):
            rows = pl.ds(k * part, part)
            if waits:
                core_copy(k).wait_recv()
            own = c_own[rows].reshape(part * modes, rank)
            oth = c_oth[rows].reshape(part * modes, rank)
            image = dot(own, own_in) + dot(oth, oth_in)
            y_buf[rows] = image.reshape(part, modes, rank)
            gram = gram + dot(image, image, ((0,), (0,)))
        g_part[...] = gram
        for d in range(1, n_split):
            gram_copy(d).start()
        if waits:
            for k in range(CHUNKS):
                core_copy(k).wait_send()
            pl.semaphore_signal(go_sem, inc=1, device_id=(q, p + 1, y), device_id_type=MESH)
        flat = y_buf[...].reshape(rank * modes, rank)
        x_part[:, :rank] = dot(flat, c_own[...].reshape(rank * modes, rank), ((0,), (0,)))
        x_part[:, rank:] = dot(flat, c_oth[...].reshape(rank * modes, rank), ((0,), (0,)))
        for d in range(1, n_split):
            cross_copy(d).start()
        for d in range(1, n_split):
            gram_copy(d).wait_recv()
            gram = gram + g_in[d - 1]
        eye = (
            lax.broadcasted_iota(jnp.int32, (rank, rank), 0)
            == lax.broadcasted_iota(jnp.int32, (rank, rank), 1)
        )
        diagonal = jnp.where(eye, gram, 0.0)
        trace = jnp.sum(jnp.sum(diagonal, axis=0, keepdims=True), axis=1, keepdims=True)
        shifted = gram + jnp.where(eye, SHIFT_RATIO * trace / rank, 0.0)
        lower_inverse(shifted, inv)
        inverse = inv[...]
        cross = x_part[...]
        for d in range(1, n_split):
            cross_copy(d).wait_recv()
            cross = cross + x_in[d - 1]
        carry_out[...] = dot(inverse, cross)
        carry_copy().start()
        ortho = dot(flat, inverse * scale, ((1,), (1,)))
        out_ref[...] = ortho.reshape(rank, modes, rank)
        for d in range(1, n_split):
            gram_copy(d).wait_send()
            cross_copy(d).wait_send()
        carry_copy().wait_send()

    @pl.when(p == 0)
    def _():
        send_core()
        local.wait()
        receive_sketch()
        compress(True)

    if depth > 2:
        @pl.when((p > 0) & (p < last))
        def _():
            receive_sketch()
            send_sketch(False)
            pl.semaphore_wait(go_sem, 1)
            send_core()
            for k in range(CHUNKS):
                core_copy(k).wait_recv()
            for k in range(CHUNKS):
                core_copy(k).wait_send()
            pl.semaphore_signal(go_sem, inc=1, device_id=(q, p + 1, y), device_id_type=MESH)
            finish_sketch()
            carry_copy().wait_recv()
            for i in range(modes):
                c_own[:, i, :] = dot(carry_in[:, :rank], c_own[:, i, :])
                c_oth[:, i, :] = dot(carry_in[:, rank:], c_oth[:, i, :])
            compress(False)

    @pl.when(p == last)
    def _():
        send_sketch(True)
        pl.semaphore_wait(go_sem, 1)
        send_core()
        for k in range(CHUNKS):
            core_copy(k).wait_recv()
        top = jnp.concatenate([c_own[:, i, :] for i in range(modes)], axis=1)
        bottom = jnp.concatenate([c_oth[:, i, :] for i in range(modes)], axis=1)
        joined = jnp.concatenate([top, bottom], axis=0)
        finish_sketch()
        for k in range(CHUNKS):
            core_copy(k).wait_send()
        carry_copy().wait_recv()
        moved = dot(carry_in[...] * scale, joined)
        for i in range(modes):
            out_ref[:, i, :] = moved[:, i * rank : (i + 1) * rank]


def body(n_pair, depth, n_split, summand_cores, sketch_cores):
    own_core, sketch_core = summand_cores[0, 0], sketch_cores[0]
    rank, modes, _ = own_core.shape
    scale = (rank * modes * n_split) ** 0.5
    square, wide = (rank, rank), (rank, 2 * rank)
    others = n_split - 1
    vmem = lambda *shape: pltpu.VMEM(shape, jnp.float32)
    sems = lambda *shape: pltpu.SemaphoreType.DMA(shape)
    out = pl.pallas_call(
        functools.partial(kernel, n_pair, depth, n_split, n_pair // 4, scale),
        out_shape=jax.ShapeDtypeStruct(own_core.shape, jnp.float32),
        in_specs=[pl.BlockSpec(memory_space=pl.ANY), pl.BlockSpec(memory_space=pltpu.VMEM)],
        out_specs=pl.BlockSpec(memory_space=pltpu.VMEM),
        scratch_shapes=[
            vmem(*own_core.shape), vmem(*own_core.shape), vmem(*own_core.shape), vmem(*own_core.shape),
            vmem(*square), vmem(2, n_split, *square),
            vmem(*square), vmem(others, *square),
            vmem(*wide), vmem(others, *wide),
            vmem(*square), vmem(*wide), vmem(*wide),
            pltpu.SemaphoreType.DMA,
            sems(CHUNKS), sems(CHUNKS),
            sems(2, n_split), sems(2, n_split),
            sems(others), sems(others),
            sems(others), sems(others),
            pltpu.SemaphoreType.DMA, pltpu.SemaphoreType.DMA,
            pltpu.SemaphoreType.REGULAR,
        ],
        compiler_params=pltpu.CompilerParams(
            collective_id=0, has_side_effects=True, vmem_limit_bytes=32 * 1024 * 1024
        ),
    )(own_core, sketch_core)
    return out[None, None]


def solution(mesh):
    in_specs = (P("pair", "cores", None, "split", None), P("cores", None, "split", None))
    out_specs = P("pair", "cores", None, "split", None)
    inner = functools.partial(body, mesh.shape["pair"], mesh.shape["cores"], mesh.shape["split"])
    return jax.shard_map(inner, mesh=mesh, in_specs=in_specs, out_specs=out_specs, check_vma=False)
```

```python
import functools

import jax
import jax.numpy as jnp
from jax import lax
from jax.experimental import pallas as pl
from jax.experimental.pallas import tpu as pltpu
from jax.sharding import PartitionSpec as P

SHIFT_RATIO = 0.01
CHUNKS = 8
PANEL = 8
MESH = pl.DeviceIdType.MESH


def dot(a, b, dims=((1,), (0,))):
    return lax.dot_general(
        a, b, (dims, ((), ())), precision=lax.Precision.HIGHEST, preferred_element_type=jnp.float32
    )


def lower_inverse(shifted, inv_ref):
    n = shifted.shape[0]
    lane = lax.broadcasted_iota(jnp.int32, (1, n), 1)
    state = shifted
    top = 0
    for start in range(0, n, PANEL):
        inside = (lane >= start) & (lane < start + PANEL)
        cols, rows = [], []
        for j in range(start, start + PANEL):
            cols.append(jnp.broadcast_to(state[:, j : j + 1], state.shape))
            row = state[j - top : j - top + 1, :]
            rows.append(jnp.where(inside, jnp.where(lane == j, 1.0, 0.0), row))
        scaled = []
        for k in range(PANEL):
            at = start + k - top
            pivot = cols[k][at : at + 1, :]
            recip = 1.0 / pivot
            scaled.append(rows[k] * recip)
            for m in range(k + 1, PANEL):
                factor = cols[m][at : at + 1, :] * recip
                cols[m] = cols[m] - cols[k] * factor
                rows[m] = rows[m] - rows[k] * factor
            root = lax.rsqrt(pivot)
            root = root * (1.5 - 0.5 * pivot * root * root)
            inv_ref[start + k : start + k + 1, :] = jnp.where(lane <= start + k, rows[k] * root, 0.0)
        new_top = (start + PANEL) // 8 * 8
        if start + PANEL < n:
            drop = new_top - top
            update = jnp.where(inside, 0.0, state[drop:, :])
            for k in range(PANEL):
                update = update - cols[k][drop:, :] * scaled[k]
            state, top = update, new_top


def kernel(
    n_pair, depth, n_split, stride, scale,
    c_ref, sk_ref, out_ref,
    c_own, c_oth, sk16, sk32, y_buf, s_part, s_in, g_part, g_in, g_prev, x_part, x_prev, inv,
    local_sem, local_sk_sem, c_send, c_recv, s_send, s_recv, g_send, g_recv, h_send, h_recv, x_send, x_recv, go_sem,
):
    q = lax.axis_index("pair")
    p = lax.axis_index("cores")
    y = lax.axis_index("split")
    rank, modes, _ = c_own.shape
    last = depth - 1
    before = lax.rem(q - stride + n_pair, n_pair)
    after = lax.rem(q + stride, n_pair)

    def mate(d):
        return lax.rem(y + d + n_split, n_split)

    local = pltpu.make_async_copy(c_ref, c_own, local_sem)
    local.start()
    local_sk = pltpu.make_async_copy(sk_ref, sk16, local_sk_sem)
    local_sk.start()

    barrier = pltpu.get_barrier_semaphore()

    def greet(*place):
        pl.semaphore_signal(barrier, inc=1, device_id=place, device_id_type=MESH)

    greet(after, p, y)

    @pl.when(p < last)
    def _():
        for d in range(n_split):
            greet(q, p + 1, mate(d))
            greet(after, p + 1, mate(d))
        for d in range(1, n_split):
            greet(q, p, mate(-d))

    @pl.when(p > 0)
    def _():
        for d in range(n_split):
            greet(q, p - 1, mate(-d))

    @pl.when(p == 0)
    def _():
        pl.semaphore_wait(barrier, 1 + (n_split - 1) + n_split)

    if depth > 2:
        @pl.when((p > 0) & (p < last))
        def _():
            pl.semaphore_wait(barrier, 1 + (n_split - 1) + 3 * n_split)

    @pl.when(p == last)
    def _():
        pl.semaphore_wait(barrier, 1 + 2 * n_split)

    part = rank // CHUNKS

    def core_copy(k):
        rows = pl.ds(k * part, part)
        return pltpu.make_async_remote_copy(
            src_ref=c_ref.at[rows], dst_ref=c_oth.at[rows], send_sem=c_send.at[k], recv_sem=c_recv.at[k],
            device_id=(before, p, y), device_id_type=MESH,
        )

    def sketch_copy(which, d):
        return pltpu.make_async_remote_copy(
            src_ref=s_part, dst_ref=s_in.at[which, d],
            send_sem=s_send.at[which, d], recv_sem=s_recv.at[which, d],
            device_id=(q if which == 0 else before, p - 1, mate(d)), device_id_type=MESH,
        )

    def gram_copy(d):
        return pltpu.make_async_remote_copy(
            src_ref=g_part, dst_ref=g_in.at[d - 1], send_sem=g_send.at[d - 1], recv_sem=g_recv.at[d - 1],
            device_id=(q, p, mate(d)), device_id_type=MESH,
        )

    def gram_on_copy(d):
        return pltpu.make_async_remote_copy(
            src_ref=g_part, dst_ref=g_prev.at[d], send_sem=h_send.at[d], recv_sem=h_recv.at[d],
            device_id=(q, p + 1, mate(d)), device_id_type=MESH,
        )

    def cross_copy(d):
        return pltpu.make_async_remote_copy(
            src_ref=x_part, dst_ref=x_prev.at[d], send_sem=x_send.at[d], recv_sem=x_recv.at[d],
            device_id=(q, p + 1, mate(d)), device_id_type=MESH,
        )

    def send_core():
        for k in range(CHUNKS):
            core_copy(k).start()

    def receive_sketch(which):
        for d in range(n_split):
            sketch_copy(which, d).wait_recv()
        total = s_in[which, 0]
        for d in range(1, n_split):
            total = total + s_in[which, d]
        s_in[which, 0] = total

    def send_sketch(at_end):
        local_sk.wait()
        sk32[...] = sk16[...].astype(jnp.float32)
        local.wait()
        if at_end:
            left = jnp.concatenate([c_own[:, i, :] for i in range(modes)], axis=1)
        else:
            inner = dot(c_own[...].reshape(rank * modes, rank), s_in[0, 0])
            y_buf[...] = inner.reshape(rank, modes, rank)
            left = jnp.concatenate([y_buf[:, i, :] for i in range(modes)], axis=1)
        right = jnp.concatenate([sk32[:, i, :] for i in range(modes)], axis=1)
        s_part[...] = dot(left, right, ((1,), (1,)))
        for which in (1, 0):
            for d in range(n_split):
                sketch_copy(which, d).start()

    def finish_sketch():
        for which in range(2):
            for d in range(n_split):
                sketch_copy(which, d).wait_send()

    def pass_turn():
        pl.semaphore_signal(go_sem, inc=1, device_id=(q, p + 1, y), device_id_type=MESH)

    def factor(gram):
        eye = (
            lax.broadcasted_iota(jnp.int32, (rank, rank), 0)
            == lax.broadcasted_iota(jnp.int32, (rank, rank), 1)
        )
        diagonal = jnp.where(eye, gram, 0.0)
        trace = jnp.sum(jnp.sum(diagonal, axis=0, keepdims=True), axis=1, keepdims=True)
        lower_inverse(gram + jnp.where(eye, SHIFT_RATIO * trace / rank, 0.0), inv)
        return inv[...]

    def carry_of_previous():
        for d in range(n_split):
            gram_on_copy(d).wait_recv()
        gram = g_prev[0]
        for d in range(1, n_split):
            gram = gram + g_prev[d]
        inverse = factor(gram)
        for d in range(n_split):
            cross_copy(d).wait_recv()
        cross = x_prev[0]
        for d in range(1, n_split):
            cross = cross + x_prev[d]
        return dot(inverse, cross)

    def compress(first):
        flat = (rank * modes, rank)
        if first:
            receive_sketch(0)
        y_buf[...] = dot(c_own[...].reshape(flat), s_in[0, 0]).reshape(c_own.shape)
        if first:
            receive_sketch(1)
        oth_in = s_in[1, 0]
        gram = jnp.zeros((rank, rank), jnp.float32)
        for k in range(CHUNKS):
            rows = pl.ds(k * part, part)
            if first:
                if k == CHUNKS - 1:
                    for m in range(CHUNKS - 1):
                        core_copy(m).wait_send()
                    pass_turn()
                core_copy(k).wait_recv()
            oth = c_oth[rows].reshape(part * modes, rank)
            image = y_buf[rows].reshape(part * modes, rank) + dot(oth, oth_in)
            y_buf[rows] = image.reshape(part, modes, rank)
            gram = gram + dot(image, image, ((0,), (0,)))
        g_part[...] = gram
        for d in range(1, n_split):
            gram_copy(d).start()
        for d in range(n_split):
            gram_on_copy(d).start()
        if first:
            core_copy(CHUNKS - 1).wait_send()
        image = y_buf[...].reshape(flat)
        x_part[:, :rank] = dot(image, c_own[...].reshape(flat), ((0,), (0,)))
        x_part[:, rank:] = dot(image, c_oth[...].reshape(flat), ((0,), (0,)))
        for d in range(n_split):
            cross_copy(d).start()
        total = gram
        for d in range(1, n_split):
            gram_copy(d).wait_recv()
            total = total + g_in[d - 1]
        inverse = factor(total)
        ortho = dot(image, inverse * scale, ((1,), (1,)))
        out_ref[...] = ortho.reshape(rank, modes, rank)
        for d in range(1, n_split):
            gram_copy(d).wait_send()
        for d in range(n_split):
            gram_on_copy(d).wait_send()
            cross_copy(d).wait_send()

    @pl.when(p == 0)
    def _():
        send_core()
        local_sk.wait()
        local.wait()
        compress(True)

    if depth > 2:
        @pl.when((p > 0) & (p < last))
        def _():
            receive_sketch(0)
            receive_sketch(1)
            send_sketch(False)
            pl.semaphore_wait(go_sem, 1)
            send_core()
            for k in range(CHUNKS):
                core_copy(k).wait_recv()
            for k in range(CHUNKS):
                core_copy(k).wait_send()
            pass_turn()
            finish_sketch()
            carry = carry_of_previous()
            for i in range(modes):
                c_own[:, i, :] = dot(carry[:, :rank], c_own[:, i, :])
                c_oth[:, i, :] = dot(carry[:, rank:], c_oth[:, i, :])
            compress(False)

    @pl.when(p == last)
    def _():
        send_sketch(True)
        pl.semaphore_wait(go_sem, 1)
        send_core()
        carry = carry_of_previous() * scale
        finish_sketch()
        top = jnp.concatenate([c_own[:, i, :] for i in range(modes)], axis=1)
        moved = dot(carry[:, :rank], top)
        for k in range(CHUNKS):
            core_copy(k).wait_recv()
        bottom = jnp.concatenate([c_oth[:, i, :] for i in range(modes)], axis=1)
        moved = moved + dot(carry[:, rank:], bottom)
        for i in range(modes):
            out_ref[:, i, :] = moved[:, i * rank : (i + 1) * rank]
        for k in range(CHUNKS):
            core_copy(k).wait_send()


def body(n_pair, depth, n_split, summand_cores, sketch_cores):
    own_core, sketch_core = summand_cores[0, 0], sketch_cores[0]
    rank, modes, _ = own_core.shape
    scale = (rank * modes * n_split) ** 0.5
    square, wide = (rank, rank), (rank, 2 * rank)
    others = n_split - 1
    vmem = lambda *shape: pltpu.VMEM(shape, jnp.float32)
    sems = lambda *shape: pltpu.SemaphoreType.DMA(shape)
    out = pl.pallas_call(
        functools.partial(kernel, n_pair, depth, n_split, n_pair // 4, scale),
        out_shape=jax.ShapeDtypeStruct(own_core.shape, jnp.float32),
        in_specs=[pl.BlockSpec(memory_space=pltpu.HBM)] * 2,
        out_specs=pl.BlockSpec(memory_space=pltpu.VMEM),
        scratch_shapes=[
            vmem(*own_core.shape), vmem(*own_core.shape),
            pltpu.VMEM(sketch_core.shape, sketch_core.dtype), vmem(*sketch_core.shape), vmem(*own_core.shape),
            vmem(*square), vmem(2, n_split, *square),
            vmem(*square), vmem(others, *square), vmem(n_split, *square),
            vmem(*wide), vmem(n_split, *wide),
            vmem(*square),
            pltpu.SemaphoreType.DMA, pltpu.SemaphoreType.DMA,
            sems(CHUNKS), sems(CHUNKS),
            sems(2, n_split), sems(2, n_split),
            sems(others), sems(others),
            sems(n_split), sems(n_split),
            sems(n_split), sems(n_split),
            pltpu.SemaphoreType.REGULAR,
        ],
        compiler_params=pltpu.CompilerParams(
            collective_id=0, has_side_effects=True, vmem_limit_bytes=65000 * 1024
        ),
    )(own_core, sketch_core)
    return out[None, None]


def solution(mesh):
    in_specs = (P("pair", "cores", None, "split", None), P("cores", None, "split", None))
    out_specs = P("pair", "cores", None, "split", None)
    inner = functools.partial(body, mesh.shape["pair"], mesh.shape["cores"], mesh.shape["split"])
    return jax.shard_map(inner, mesh=mesh, in_specs=in_specs, out_specs=out_specs, check_vma=False)
```

```python
import functools

import jax
import jax.numpy as jnp
from jax import lax
from jax.experimental import pallas as pl
from jax.experimental.pallas import tpu as pltpu
from jax.sharding import PartitionSpec as P

SHIFT_RATIO = 0.01
CHUNKS = 4
PANEL = 8
MESH = pl.DeviceIdType.MESH


def dot(a, b, dims=((1,), (0,))):
    return lax.dot_general(
        a, b, (dims, ((), ())), precision=lax.Precision.HIGHEST, preferred_element_type=jnp.float32
    )


def dot_exact_right(a, b):
    total = None
    for _ in range(3):
        term = a.astype(jnp.bfloat16)
        a = a - term.astype(jnp.float32)
        piece = lax.dot_general(
            term, b, (((1,), (1,)), ((), ())), preferred_element_type=jnp.float32
        )
        total = piece if total is None else total + piece
    return total


def lower_inverse(shifted, inv_ref):
    n = shifted.shape[0]
    lane = lax.broadcasted_iota(jnp.int32, (1, n), 1)
    state = shifted
    top = 0
    for start in range(0, n, PANEL):
        inside = (lane >= start) & (lane < start + PANEL)
        cols, rows = [], []
        for j in range(start, start + PANEL):
            cols.append(jnp.broadcast_to(state[:, j : j + 1], state.shape))
            row = state[j - top : j - top + 1, :]
            rows.append(jnp.where(inside, jnp.where(lane == j, 1.0, 0.0), row))
        scaled = []
        for k in range(PANEL):
            at = start + k - top
            pivot = cols[k][at : at + 1, :]
            recip = 1.0 / pivot
            scaled.append(rows[k] * recip)
            for m in range(k + 1, PANEL):
                factor = cols[m][at : at + 1, :] * recip
                cols[m] = cols[m] - cols[k] * factor
                rows[m] = rows[m] - rows[k] * factor
            root = lax.rsqrt(pivot)
            root = root * (1.5 - 0.5 * pivot * root * root)
            inv_ref[start + k : start + k + 1, :] = jnp.where(lane <= start + k, rows[k] * root, 0.0)
        new_top = (start + PANEL) // 8 * 8
        if start + PANEL < n:
            drop = new_top - top
            update = jnp.where(inside, 0.0, state[drop:, :])
            for k in range(PANEL):
                update = update - cols[k][drop:, :] * scaled[k]
            state, top = update, new_top


def kernel(
    n_pair, depth, n_split, stride, scale,
    c_ref, sk_ref, out_ref,
    c_own, c_oth, sk16, sk32, y_buf, s_part, s_in, g_part, g_in, g_prev, x_part, x_prev, inv,
    local_sem, local_sk_sem, c_send, c_recv, s_send, s_recv, g_send, g_recv, h_send, h_recv, x_send, x_recv, go_sem,
):
    q = lax.axis_index("pair")
    p = lax.axis_index("cores")
    y = lax.axis_index("split")
    rank, modes, _ = c_own.shape
    last = depth - 1
    before = lax.rem(q - stride + n_pair, n_pair)
    after = lax.rem(q + stride, n_pair)

    def mate(d):
        return lax.rem(y + d + n_split, n_split)

    local = pltpu.make_async_copy(c_ref, c_own, local_sem)
    local.start()
    local_sk = pltpu.make_async_copy(sk_ref, sk16, local_sk_sem)
    local_sk.start()

    barrier = pltpu.get_barrier_semaphore()

    def greet(*place):
        pl.semaphore_signal(barrier, inc=1, device_id=place, device_id_type=MESH)

    greet(after, p, y)

    @pl.when(p < last)
    def _():
        for d in range(n_split):
            greet(q, p + 1, mate(d))
            greet(after, p + 1, mate(d))
        for d in range(1, n_split):
            greet(q, p, mate(-d))

    @pl.when(p > 0)
    def _():
        for d in range(n_split):
            greet(q, p - 1, mate(-d))

    @pl.when(p == 0)
    def _():
        pl.semaphore_wait(barrier, 1 + (n_split - 1) + n_split)

    if depth > 2:
        @pl.when((p > 0) & (p < last))
        def _():
            pl.semaphore_wait(barrier, 1 + (n_split - 1) + 3 * n_split)

    @pl.when(p == last)
    def _():
        pl.semaphore_wait(barrier, 1 + 2 * n_split)

    part = rank // CHUNKS

    def core_copy(k):
        rows = pl.ds(k * part, part)
        return pltpu.make_async_remote_copy(
            src_ref=c_ref.at[rows], dst_ref=c_oth.at[rows], send_sem=c_send.at[k], recv_sem=c_recv.at[k],
            device_id=(before, p, y), device_id_type=MESH,
        )

    def sketch_copy(which, d):
        return pltpu.make_async_remote_copy(
            src_ref=s_part, dst_ref=s_in.at[which, d],
            send_sem=s_send.at[which, d], recv_sem=s_recv.at[which, d],
            device_id=(q if which == 0 else before, p - 1, mate(d)), device_id_type=MESH,
        )

    def gram_copy(d):
        return pltpu.make_async_remote_copy(
            src_ref=g_part, dst_ref=g_in.at[d - 1], send_sem=g_send.at[d - 1], recv_sem=g_recv.at[d - 1],
            device_id=(q, p, mate(d)), device_id_type=MESH,
        )

    def gram_on_copy(d):
        return pltpu.make_async_remote_copy(
            src_ref=g_part, dst_ref=g_prev.at[d], send_sem=h_send.at[d], recv_sem=h_recv.at[d],
            device_id=(q, p + 1, mate(d)), device_id_type=MESH,
        )

    def cross_copy(d):
        return pltpu.make_async_remote_copy(
            src_ref=x_part, dst_ref=x_prev.at[d], send_sem=x_send.at[d], recv_sem=x_recv.at[d],
            device_id=(q, p + 1, mate(d)), device_id_type=MESH,
        )

    def send_core():
        for k in range(CHUNKS):
            core_copy(k).start()

    def receive_sketch(which):
        for d in range(n_split):
            sketch_copy(which, d).wait_recv()
        total = s_in[which, 0]
        for d in range(1, n_split):
            total = total + s_in[which, d]
        s_in[which, 0] = total

    def send_sketch(at_end):
        local_sk.wait()
        sk32[...] = sk16[...].astype(jnp.float32)
        local.wait()
        if at_end:
            left = jnp.concatenate([c_own[:, i, :] for i in range(modes)], axis=1)
        else:
            inner = dot(c_own[...].reshape(rank * modes, rank), s_in[0, 0])
            y_buf[...] = inner.reshape(rank, modes, rank)
            left = jnp.concatenate([y_buf[:, i, :] for i in range(modes)], axis=1)
        right = jnp.concatenate([sk32[:, i, :] for i in range(modes)], axis=1)
        s_part[...] = dot_exact_right(left, right.astype(jnp.bfloat16))
        for which in (1, 0):
            for d in range(n_split):
                sketch_copy(which, d).start()

    def finish_sketch():
        for which in range(2):
            for d in range(n_split):
                sketch_copy(which, d).wait_send()

    def pass_turn():
        pl.semaphore_signal(go_sem, inc=1, device_id=(q, p + 1, y), device_id_type=MESH)

    def factor(gram):
        eye = (
            lax.broadcasted_iota(jnp.int32, (rank, rank), 0)
            == lax.broadcasted_iota(jnp.int32, (rank, rank), 1)
        )
        diagonal = jnp.where(eye, gram, 0.0)
        trace = jnp.sum(jnp.sum(diagonal, axis=0, keepdims=True), axis=1, keepdims=True)
        lower_inverse(gram + jnp.where(eye, SHIFT_RATIO * trace / rank, 0.0), inv)
        return inv[...]

    def carry_of_previous():
        for d in range(n_split):
            gram_on_copy(d).wait_recv()
        gram = g_prev[0]
        for d in range(1, n_split):
            gram = gram + g_prev[d]
        inverse = factor(gram)
        for d in range(n_split):
            cross_copy(d).wait_recv()
        cross = x_prev[0]
        for d in range(1, n_split):
            cross = cross + x_prev[d]
        return dot(inverse, cross)

    def compress(first):
        if first:
            receive_sketch(0)
            receive_sketch(1)
        g_part[...] = jnp.zeros(g_part.shape, jnp.float32)
        x_part[...] = jnp.zeros(x_part.shape, jnp.float32)

        def chunk_turn(k, _):
            rows = pl.ds(k * part, part)
            if first:
                @pl.when(k == CHUNKS - 1)
                def _():
                    for m in range(CHUNKS - 1):
                        core_copy(m).wait_send()
                    pass_turn()

                core_copy(k).wait_recv()
            own = c_own[rows].reshape(part * modes, rank)
            oth = c_oth[rows].reshape(part * modes, rank)
            image = dot(own, s_in[0, 0]) + dot(oth, s_in[1, 0])
            y_buf[rows] = image.reshape(part, modes, rank)
            flipped = image.T
            g_part[...] += dot(flipped, image)
            x_part[:, :rank] += dot(flipped, own)
            x_part[:, rank:] += dot(flipped, oth)
            return 0

        lax.fori_loop(0, CHUNKS, chunk_turn, 0)
        for d in range(1, n_split):
            gram_copy(d).start()
        for d in range(n_split):
            gram_on_copy(d).start()
        for d in range(n_split):
            cross_copy(d).start()
        if first:
            core_copy(CHUNKS - 1).wait_send()
        total = g_part[...]
        for d in range(1, n_split):
            gram_copy(d).wait_recv()
            total = total + g_in[d - 1]
        inverse = (factor(total) * scale).T

        def ortho_turn(k, _):
            rows = pl.ds(k * part, part)
            image = y_buf[rows].reshape(part * modes, rank)
            out_ref[rows] = dot(image, inverse).reshape(part, modes, rank)
            return 0

        lax.fori_loop(0, CHUNKS, ortho_turn, 0)
        for d in range(1, n_split):
            gram_copy(d).wait_send()
        for d in range(n_split):
            gram_on_copy(d).wait_send()
            cross_copy(d).wait_send()

    @pl.when(p == 0)
    def _():
        send_core()
        local_sk.wait()
        local.wait()
        compress(True)

    if depth > 2:
        @pl.when((p > 0) & (p < last))
        def _():
            receive_sketch(0)
            receive_sketch(1)
            send_sketch(False)
            pl.semaphore_wait(go_sem, 1)
            send_core()
            for k in range(CHUNKS):
                core_copy(k).wait_recv()
            for k in range(CHUNKS):
                core_copy(k).wait_send()
            pass_turn()
            finish_sketch()
            carry = carry_of_previous()
            for i in range(modes):
                c_own[:, i, :] = dot(carry[:, :rank], c_own[:, i, :])
                c_oth[:, i, :] = dot(carry[:, rank:], c_oth[:, i, :])
            compress(False)

    @pl.when(p == last)
    def _():
        send_sketch(True)
        pl.semaphore_wait(go_sem, 1)
        send_core()
        carry = carry_of_previous() * scale
        finish_sketch()
        top = jnp.concatenate([c_own[:, i, :] for i in range(modes)], axis=1)
        moved = dot(carry[:, :rank], top)
        for k in range(CHUNKS):
            core_copy(k).wait_recv()
        bottom = jnp.concatenate([c_oth[:, i, :] for i in range(modes)], axis=1)
        moved = moved + dot(carry[:, rank:], bottom)
        for i in range(modes):
            out_ref[:, i, :] = moved[:, i * rank : (i + 1) * rank]
        for k in range(CHUNKS):
            core_copy(k).wait_send()


def body(n_pair, depth, n_split, summand_cores, sketch_cores):
    own_core, sketch_core = summand_cores[0, 0], sketch_cores[0]
    rank, modes, _ = own_core.shape
    scale = (rank * modes * n_split) ** 0.5
    square, wide = (rank, rank), (rank, 2 * rank)
    others = n_split - 1
    vmem = lambda *shape: pltpu.VMEM(shape, jnp.float32)
    sems = lambda *shape: pltpu.SemaphoreType.DMA(shape)
    out = pl.pallas_call(
        functools.partial(kernel, n_pair, depth, n_split, n_pair // 4, scale),
        out_shape=jax.ShapeDtypeStruct(own_core.shape, jnp.float32),
        in_specs=[pl.BlockSpec(memory_space=pltpu.HBM)] * 2,
        out_specs=pl.BlockSpec(memory_space=pltpu.VMEM),
        scratch_shapes=[
            vmem(*own_core.shape), vmem(*own_core.shape),
            pltpu.VMEM(sketch_core.shape, sketch_core.dtype), vmem(*sketch_core.shape), vmem(*own_core.shape),
            vmem(*square), vmem(2, n_split, *square),
            vmem(*square), vmem(others, *square), vmem(n_split, *square),
            vmem(*wide), vmem(n_split, *wide),
            vmem(*square),
            pltpu.SemaphoreType.DMA, pltpu.SemaphoreType.DMA,
            sems(CHUNKS), sems(CHUNKS),
            sems(2, n_split), sems(2, n_split),
            sems(others), sems(others),
            sems(n_split), sems(n_split),
            sems(n_split), sems(n_split),
            pltpu.SemaphoreType.REGULAR,
        ],
        compiler_params=pltpu.CompilerParams(
            collective_id=0, has_side_effects=True, vmem_limit_bytes=65000 * 1024
        ),
    )(own_core, sketch_core)
    return out[None, None]


def solution(mesh):
    in_specs = (P("pair", "cores", None, "split", None), P("cores", None, "split", None))
    out_specs = P("pair", "cores", None, "split", None)
    inner = functools.partial(body, mesh.shape["pair"], mesh.shape["cores"], mesh.shape["split"])
    return jax.shard_map(inner, mesh=mesh, in_specs=in_specs, out_specs=out_specs, check_vma=False)
```

```python
import functools

import jax
import jax.numpy as jnp
from jax import lax
from jax.experimental import pallas as pl
from jax.experimental.pallas import tpu as pltpu
from jax.sharding import PartitionSpec as P

SHIFT_RATIO = 0.01
CHUNKS = 8
PANEL = 8
MESH = pl.DeviceIdType.MESH


def dot(a, b, dims=((1,), (0,))):
    return lax.dot_general(
        a, b, (dims, ((), ())), precision=lax.Precision.HIGHEST, preferred_element_type=jnp.float32
    )


def dot_exact_right(a, b):
    total = None
    for _ in range(3):
        term = a.astype(jnp.bfloat16)
        a = a - term.astype(jnp.float32)
        piece = lax.dot_general(
            term, b, (((1,), (1,)), ((), ())), preferred_element_type=jnp.float32
        )
        total = piece if total is None else total + piece
    return total


def lower_inverse(shifted, inv_ref):
    n = shifted.shape[0]
    lane = lax.broadcasted_iota(jnp.int32, (1, n), 1)
    state = shifted
    top = 0
    for start in range(0, n, PANEL):
        inside = (lane >= start) & (lane < start + PANEL)
        cols, rows = [], []
        for j in range(start, start + PANEL):
            cols.append(jnp.broadcast_to(state[:, j : j + 1], state.shape))
            row = state[j - top : j - top + 1, :]
            rows.append(jnp.where(inside, jnp.where(lane == j, 1.0, 0.0), row))
        scaled = []
        for k in range(PANEL):
            at = start + k - top
            pivot = cols[k][at : at + 1, :]
            recip = 1.0 / pivot
            scaled.append(rows[k] * recip)
            for m in range(k + 1, PANEL):
                factor = cols[m][at : at + 1, :] * recip
                cols[m] = cols[m] - cols[k] * factor
                rows[m] = rows[m] - rows[k] * factor
            root = lax.rsqrt(pivot)
            root = root * (1.5 - 0.5 * pivot * root * root)
            inv_ref[start + k : start + k + 1, :] = jnp.where(lane <= start + k, rows[k] * root, 0.0)
        new_top = (start + PANEL) // 8 * 8
        if start + PANEL < n:
            drop = new_top - top
            update = jnp.where(inside, 0.0, state[drop:, :])
            for k in range(PANEL):
                update = update - cols[k][drop:, :] * scaled[k]
            state, top = update, new_top


def kernel(
    n_pair, depth, n_split, stride,
    c_ref, sk_ref, out_ref,
    c_own, c_oth, sk16, sk32, y_buf, s_part, s_in, g_part, g_in, g_prev, x_part, x_prev, inv,
    local_sem, local_sk_sem, c_send, c_recv, s_send, s_recv, g_send, g_recv, h_send, h_recv, x_send, x_recv, go_sem,
):
    q = lax.axis_index("pair")
    p = lax.axis_index("cores")
    y = lax.axis_index("split")
    rank, modes, _ = c_own.shape
    last = depth - 1
    before = lax.rem(q - stride + n_pair, n_pair)
    after = lax.rem(q + stride, n_pair)

    def mate(d):
        return lax.rem(y + d + n_split, n_split)

    local = pltpu.make_async_copy(c_ref, c_own, local_sem)
    local.start()
    local_sk = pltpu.make_async_copy(sk_ref, sk16, local_sk_sem)
    local_sk.start()

    barrier = pltpu.get_barrier_semaphore()

    def greet(*place):
        pl.semaphore_signal(barrier, inc=1, device_id=place, device_id_type=MESH)

    greet(after, p, y)

    @pl.when(p < last)
    def _():
        for d in range(n_split):
            greet(q, p + 1, mate(d))
            greet(after, p + 1, mate(d))
        for d in range(1, n_split):
            greet(q, p, mate(-d))

    @pl.when(p > 0)
    def _():
        for d in range(n_split):
            greet(q, p - 1, mate(-d))

    def make_sketch(at_end):
        local_sk.wait()
        sk32[...] = sk16[...].astype(jnp.float32)
        local.wait()
        if at_end:
            left = jnp.concatenate([c_own[:, i, :] for i in range(modes)], axis=1)
        else:
            inner = dot(c_own[...].reshape(rank * modes, rank), s_in[0, 0])
            y_buf[...] = inner.reshape(rank, modes, rank)
            left = jnp.concatenate([y_buf[:, i, :] for i in range(modes)], axis=1)
        right = jnp.concatenate([sk32[:, i, :] for i in range(modes)], axis=1)
        s_part[...] = dot_exact_right(left, right.astype(jnp.bfloat16))

    @pl.when(p == last)
    def _():
        make_sketch(True)

    @pl.when(p == 0)
    def _():
        pl.semaphore_wait(barrier, 1 + (n_split - 1) + n_split)

    if depth > 2:
        @pl.when((p > 0) & (p < last))
        def _():
            pl.semaphore_wait(barrier, 1 + (n_split - 1) + 3 * n_split)

    @pl.when(p == last)
    def _():
        pl.semaphore_wait(barrier, 1 + 2 * n_split)

    part = rank // CHUNKS

    def core_copy(k):
        rows = pl.ds(k * part, part)
        return pltpu.make_async_remote_copy(
            src_ref=c_ref.at[rows], dst_ref=c_oth.at[rows], send_sem=c_send.at[k], recv_sem=c_recv.at[k],
            device_id=(before, p, y), device_id_type=MESH,
        )

    def sketch_copy(which, d):
        return pltpu.make_async_remote_copy(
            src_ref=s_part, dst_ref=s_in.at[which, d],
            send_sem=s_send.at[which, d], recv_sem=s_recv.at[which, d],
            device_id=(q if which == 0 else before, p - 1, mate(d)), device_id_type=MESH,
        )

    def gram_copy(d):
        return pltpu.make_async_remote_copy(
            src_ref=g_part, dst_ref=g_in.at[d - 1], send_sem=g_send.at[d - 1], recv_sem=g_recv.at[d - 1],
            device_id=(q, p, mate(d)), device_id_type=MESH,
        )

    def gram_on_copy(d):
        return pltpu.make_async_remote_copy(
            src_ref=g_part, dst_ref=g_prev.at[d], send_sem=h_send.at[d], recv_sem=h_recv.at[d],
            device_id=(q, p + 1, mate(d)), device_id_type=MESH,
        )

    def cross_copy(d):
        return pltpu.make_async_remote_copy(
            src_ref=x_part, dst_ref=x_prev.at[d], send_sem=x_send.at[d], recv_sem=x_recv.at[d],
            device_id=(q, p + 1, mate(d)), device_id_type=MESH,
        )

    def send_core():
        for k in range(CHUNKS):
            core_copy(k).start()

    def receive_sketch(which):
        for d in range(n_split):
            sketch_copy(which, d).wait_recv()
        total = s_in[which, 0]
        for d in range(1, n_split):
            total = total + s_in[which, d]
        s_in[which, 0] = total

    def send_sketch():
        for which in (1, 0):
            for d in range(n_split):
                sketch_copy(which, d).start()

    def finish_sketch():
        for which in range(2):
            for d in range(n_split):
                sketch_copy(which, d).wait_send()

    def pass_turn():
        pl.semaphore_signal(go_sem, inc=1, device_id=(q, p + 1, y), device_id_type=MESH)

    def factor(gram):
        eye = (
            lax.broadcasted_iota(jnp.int32, (rank, rank), 0)
            == lax.broadcasted_iota(jnp.int32, (rank, rank), 1)
        )
        diagonal = jnp.where(eye, gram, 0.0)
        trace = jnp.sum(jnp.sum(diagonal, axis=0, keepdims=True), axis=1, keepdims=True)
        lower_inverse(gram + jnp.where(eye, SHIFT_RATIO * trace / rank, 0.0), inv)
        return inv[...]

    def carry_of_previous():
        for d in range(n_split):
            gram_on_copy(d).wait_recv()
        gram = g_prev[0]
        for d in range(1, n_split):
            gram = gram + g_prev[d]
        inverse = factor(gram)
        for d in range(n_split):
            cross_copy(d).wait_recv()
        cross = x_prev[0]
        for d in range(1, n_split):
            cross = cross + x_prev[d]
        return dot(inverse, cross)

    def compress(first):
        flat = (rank * modes, rank)
        if first:
            receive_sketch(0)
        y_buf[...] = dot(c_own[...].reshape(flat), s_in[0, 0]).reshape(c_own.shape)
        if first:
            for k in range(CHUNKS // 2):
                core_copy(k).wait_send()
            pass_turn()
            receive_sketch(1)
        oth_in = s_in[1, 0]
        gram = jnp.zeros((rank, rank), jnp.float32)
        for k in range(CHUNKS):
            rows = pl.ds(k * part, part)
            if first:
                core_copy(k).wait_recv()
            oth = c_oth[rows].reshape(part * modes, rank)
            image = y_buf[rows].reshape(part * modes, rank) + dot(oth, oth_in)
            y_buf[rows] = image.reshape(part, modes, rank)
            gram = gram + dot(image, image, ((0,), (0,)))
        g_part[...] = gram
        for d in range(1, n_split):
            gram_copy(d).start()
        for d in range(n_split):
            gram_on_copy(d).start()
        if first:
            for k in range(CHUNKS // 2, CHUNKS):
                core_copy(k).wait_send()
        image = y_buf[...].reshape(flat)
        x_part[:, :rank] = dot(image, c_own[...].reshape(flat), ((0,), (0,)))
        x_part[:, rank:] = dot(image, c_oth[...].reshape(flat), ((0,), (0,)))
        for d in range(n_split):
            cross_copy(d).start()
        total = gram
        for d in range(1, n_split):
            gram_copy(d).wait_recv()
            total = total + g_in[d - 1]
        inverse = factor(total)
        ortho = dot(image, inverse, ((1,), (1,)))
        out_ref[...] = ortho.reshape(rank, modes, rank)
        for d in range(1, n_split):
            gram_copy(d).wait_send()
        for d in range(n_split):
            gram_on_copy(d).wait_send()
            cross_copy(d).wait_send()

    @pl.when(p == 0)
    def _():
        send_core()
        local_sk.wait()
        local.wait()
        compress(True)

    if depth > 2:
        @pl.when((p > 0) & (p < last))
        def _():
            receive_sketch(0)
            receive_sketch(1)
            make_sketch(False)
            send_sketch()
            pl.semaphore_wait(go_sem, 1)
            send_core()
            for k in range(CHUNKS):
                core_copy(k).wait_recv()
            for k in range(CHUNKS):
                core_copy(k).wait_send()
            pass_turn()
            finish_sketch()
            carry = carry_of_previous()
            for i in range(modes):
                c_own[:, i, :] = dot(carry[:, :rank], c_own[:, i, :])
                c_oth[:, i, :] = dot(carry[:, rank:], c_oth[:, i, :])
            compress(False)

    @pl.when(p == last)
    def _():
        send_sketch()
        pl.semaphore_wait(go_sem, 1)
        send_core()
        carry = carry_of_previous()
        finish_sketch()
        top = jnp.concatenate([c_own[:, i, :] for i in range(modes)], axis=1)
        moved = dot(carry[:, :rank], top)
        for k in range(CHUNKS):
            core_copy(k).wait_recv()
        bottom = jnp.concatenate([c_oth[:, i, :] for i in range(modes)], axis=1)
        moved = moved + dot(carry[:, rank:], bottom)
        for i in range(modes):
            out_ref[:, i, :] = moved[:, i * rank : (i + 1) * rank]
        for k in range(CHUNKS):
            core_copy(k).wait_send()


def body(n_pair, depth, n_split, summand_cores, sketch_cores):
    own_core, sketch_core = summand_cores[0, 0], sketch_cores[0]
    rank, modes, _ = own_core.shape
    scale = (rank * modes * n_split) ** 0.5
    square, wide = (rank, rank), (rank, 2 * rank)
    others = n_split - 1
    vmem = lambda *shape: pltpu.VMEM(shape, jnp.float32)
    sems = lambda *shape: pltpu.SemaphoreType.DMA(shape)
    out = pl.pallas_call(
        functools.partial(kernel, n_pair, depth, n_split, n_pair // 4),
        out_shape=jax.ShapeDtypeStruct(own_core.shape, jnp.float32),
        in_specs=[pl.BlockSpec(memory_space=pltpu.HBM)] * 2,
        out_specs=pl.BlockSpec(memory_space=pltpu.VMEM),
        scratch_shapes=[
            vmem(*own_core.shape), vmem(*own_core.shape),
            pltpu.VMEM(sketch_core.shape, sketch_core.dtype), vmem(*sketch_core.shape), vmem(*own_core.shape),
            vmem(*square), vmem(2, n_split, *square),
            vmem(*square), vmem(others, *square), vmem(n_split, *square),
            vmem(*wide), vmem(n_split, *wide),
            vmem(*square),
            pltpu.SemaphoreType.DMA, pltpu.SemaphoreType.DMA,
            sems(CHUNKS), sems(CHUNKS),
            sems(2, n_split), sems(2, n_split),
            sems(others), sems(others),
            sems(n_split), sems(n_split),
            sems(n_split), sems(n_split),
            pltpu.SemaphoreType.REGULAR,
        ],
        compiler_params=pltpu.CompilerParams(
            collective_id=0, has_side_effects=True, vmem_limit_bytes=65000 * 1024
        ),
    )(own_core, sketch_core)
    return (out * scale)[None, None]


def solution(mesh):
    in_specs = (P("pair", "cores", None, "split", None), P("cores", None, "split", None))
    out_specs = P("pair", "cores", None, "split", None)
    inner = functools.partial(body, mesh.shape["pair"], mesh.shape["cores"], mesh.shape["split"])
    return jax.shard_map(inner, mesh=mesh, in_specs=in_specs, out_specs=out_specs, check_vma=False)
```

```python
import functools

import jax
import jax.numpy as jnp
from jax import lax
from jax.experimental import pallas as pl
from jax.experimental.pallas import tpu as pltpu
from jax.sharding import PartitionSpec as P

SHIFT_RATIO = 0.01
CHUNKS = 8
PANEL = 8
MESH = pl.DeviceIdType.MESH


def dot(a, b, dims=((1,), (0,))):
    return lax.dot_general(
        a, b, (dims, ((), ())), precision=lax.Precision.HIGHEST, preferred_element_type=jnp.float32
    )


def dot_exact_right(a, b):
    total = None
    for _ in range(3):
        term = a.astype(jnp.bfloat16)
        a = a - term.astype(jnp.float32)
        piece = lax.dot_general(
            term, b, (((1,), (1,)), ((), ())), preferred_element_type=jnp.float32
        )
        total = piece if total is None else total + piece
    return total


def lower_inverse(shifted, inv_ref):
    n = shifted.shape[0]
    lane = lax.broadcasted_iota(jnp.int32, (1, n), 1)
    state = shifted
    top = 0
    for start in range(0, n, PANEL):
        inside = (lane >= start) & (lane < start + PANEL)
        cols, rows = [], []
        for j in range(start, start + PANEL):
            cols.append(jnp.broadcast_to(state[:, j : j + 1], state.shape))
            row = state[j - top : j - top + 1, :]
            rows.append(jnp.where(inside, jnp.where(lane == j, 1.0, 0.0), row))
        scaled = []
        for k in range(PANEL):
            at = start + k - top
            pivot = cols[k][at : at + 1, :]
            recip = 1.0 / pivot
            scaled.append(rows[k] * recip)
            for m in range(k + 1, PANEL):
                factor = cols[m][at : at + 1, :] * recip
                cols[m] = cols[m] - cols[k] * factor
                rows[m] = rows[m] - rows[k] * factor
            root = lax.rsqrt(pivot)
            root = root * (1.5 - 0.5 * pivot * root * root)
            inv_ref[start + k : start + k + 1, :] = jnp.where(lane <= start + k, rows[k] * root, 0.0)
        new_top = (start + PANEL) // 8 * 8
        if start + PANEL < n:
            drop = new_top - top
            update = jnp.where(inside, 0.0, state[drop:, :])
            for k in range(PANEL):
                update = update - cols[k][drop:, :] * scaled[k]
            state, top = update, new_top


def kernel(
    n_pair, depth, n_split, stride,
    c_ref, sk_ref, out_ref,
    c_own, c_oth, sk16, sk32, y_buf, s_part, s_in, g_part, g_in, g_prev, x_part, x_prev, inv,
    local_sem, local_sk_sem, c_send, c_recv, s_send, s_recv, g_send, g_recv, h_send, h_recv, x_send, x_recv, go_sem,
):
    q = lax.axis_index("pair")
    p = lax.axis_index("cores")
    y = lax.axis_index("split")
    rank, modes, _ = c_own.shape
    last = depth - 1
    before = lax.rem(q - stride + n_pair, n_pair)
    after = lax.rem(q + stride, n_pair)

    def mate(d):
        return lax.rem(y + d + n_split, n_split)

    local = pltpu.make_async_copy(c_ref, c_own, local_sem)
    local.start()
    local_sk = pltpu.make_async_copy(sk_ref, sk16, local_sk_sem)
    local_sk.start()

    barrier = pltpu.get_barrier_semaphore()

    def greet(*place):
        pl.semaphore_signal(barrier, inc=1, device_id=place, device_id_type=MESH)

    greet(after, p, y)

    @pl.when(p < last)
    def _():
        for d in range(n_split):
            greet(q, p + 1, mate(d))
            greet(after, p + 1, mate(d))
        for d in range(1, n_split):
            greet(q, p, mate(-d))

    @pl.when(p > 0)
    def _():
        for d in range(n_split):
            greet(q, p - 1, mate(-d))

    def make_sketch(at_end):
        local_sk.wait()
        sk32[...] = sk16[...].astype(jnp.float32)
        local.wait()
        if at_end:
            left = jnp.concatenate([c_own[:, i, :] for i in range(modes)], axis=1)
        else:
            inner = dot(c_own[...].reshape(rank * modes, rank), s_in[0, 0])
            y_buf[...] = inner.reshape(rank, modes, rank)
            left = jnp.concatenate([y_buf[:, i, :] for i in range(modes)], axis=1)
        right = jnp.concatenate([sk32[:, i, :] for i in range(modes)], axis=1)
        s_part[...] = dot_exact_right(left, right.astype(jnp.bfloat16))

    @pl.when(p == last)
    def _():
        make_sketch(True)

    @pl.when(p == 0)
    def _():
        pl.semaphore_wait(barrier, 1 + (n_split - 1) + n_split)

    if depth > 2:
        @pl.when((p > 0) & (p < last))
        def _():
            pl.semaphore_wait(barrier, 1 + (n_split - 1) + 3 * n_split)

    @pl.when(p == last)
    def _():
        pl.semaphore_wait(barrier, 1 + 2 * n_split)

    part = rank // CHUNKS

    def core_copy(k):
        rows = pl.ds(k * part, part)
        return pltpu.make_async_remote_copy(
            src_ref=c_ref.at[rows], dst_ref=c_oth.at[rows], send_sem=c_send.at[k], recv_sem=c_recv.at[k],
            device_id=(before, p, y), device_id_type=MESH,
        )

    def sketch_copy(which, d):
        return pltpu.make_async_remote_copy(
            src_ref=s_part, dst_ref=s_in.at[which, d],
            send_sem=s_send.at[which, d], recv_sem=s_recv.at[which, d],
            device_id=(q if which == 0 else before, p - 1, mate(d)), device_id_type=MESH,
        )

    def gram_copy(d):
        return pltpu.make_async_remote_copy(
            src_ref=g_part, dst_ref=g_in.at[d - 1], send_sem=g_send.at[d - 1], recv_sem=g_recv.at[d - 1],
            device_id=(q, p, mate(d)), device_id_type=MESH,
        )

    def gram_on_copy(d):
        return pltpu.make_async_remote_copy(
            src_ref=g_part, dst_ref=g_prev.at[d], send_sem=h_send.at[d], recv_sem=h_recv.at[d],
            device_id=(q, p + 1, mate(d)), device_id_type=MESH,
        )

    def cross_copy(d):
        return pltpu.make_async_remote_copy(
            src_ref=x_part, dst_ref=x_prev.at[d], send_sem=x_send.at[d], recv_sem=x_recv.at[d],
            device_id=(q, p + 1, mate(d)), device_id_type=MESH,
        )

    def send_core():
        for k in range(CHUNKS):
            core_copy(k).start()

    def receive_sketch(which):
        for d in range(n_split):
            sketch_copy(which, d).wait_recv()
        total = s_in[which, 0]
        for d in range(1, n_split):
            total = total + s_in[which, d]
        s_in[which, 0] = total

    def send_sketch():
        for which in (1, 0):
            for d in range(n_split):
                sketch_copy(which, d).start()

    def finish_sketch():
        for which in range(2):
            for d in range(n_split):
                sketch_copy(which, d).wait_send()

    def pass_turn():
        pl.semaphore_signal(go_sem, inc=1, device_id=(q, p + 1, y), device_id_type=MESH)

    def factor(gram):
        eye = (
            lax.broadcasted_iota(jnp.int32, (rank, rank), 0)
            == lax.broadcasted_iota(jnp.int32, (rank, rank), 1)
        )
        diagonal = jnp.where(eye, gram, 0.0)
        trace = jnp.sum(jnp.sum(diagonal, axis=0, keepdims=True), axis=1, keepdims=True)
        lower_inverse(gram + jnp.where(eye, SHIFT_RATIO * trace / rank, 0.0), inv)
        return inv[...]

    def carry_of_previous():
        for d in range(n_split):
            gram_on_copy(d).wait_recv()
        gram = g_prev[0]
        for d in range(1, n_split):
            gram = gram + g_prev[d]
        inverse = factor(gram)
        for d in range(n_split):
            cross_copy(d).wait_recv()
        cross = x_prev[0]
        for d in range(1, n_split):
            cross = cross + x_prev[d]
        return dot(inverse, cross)

    def compress(first):
        flat = (rank * modes, rank)
        if first:
            receive_sketch(0)
        y_buf[...] = dot(c_own[...].reshape(flat), s_in[0, 0]).reshape(c_own.shape)
        if first:
            receive_sketch(1)
        oth_in = s_in[1, 0]
        gram = jnp.zeros((rank, rank), jnp.float32)
        for k in range(CHUNKS):
            rows = pl.ds(k * part, part)
            if first:
                if k == CHUNKS - 1:
                    for m in range(CHUNKS - 1):
                        core_copy(m).wait_send()
                    pass_turn()
                core_copy(k).wait_recv()
            oth = c_oth[rows].reshape(part * modes, rank)
            image = y_buf[rows].reshape(part * modes, rank) + dot(oth, oth_in)
            y_buf[rows] = image.reshape(part, modes, rank)
            gram = gram + dot(image, image, ((0,), (0,)))
        g_part[...] = gram
        for d in range(1, n_split):
            gram_copy(d).start()
        for d in range(n_split):
            gram_on_copy(d).start()
        if first:
            core_copy(CHUNKS - 1).wait_send()
        image = y_buf[...].reshape(flat)
        x_part[:, :rank] = dot(image, c_own[...].reshape(flat), ((0,), (0,)))
        x_part[:, rank:] = dot(image, c_oth[...].reshape(flat), ((0,), (0,)))
        for d in range(n_split):
            cross_copy(d).start()
        total = gram
        for d in range(1, n_split):
            gram_copy(d).wait_recv()
            total = total + g_in[d - 1]
        inverse = factor(total)
        ortho = dot(image, inverse, ((1,), (1,)))
        out_ref[...] = ortho.reshape(rank, modes, rank)
        for d in range(1, n_split):
            gram_copy(d).wait_send()
        for d in range(n_split):
            gram_on_copy(d).wait_send()
            cross_copy(d).wait_send()

    @pl.when(p == 0)
    def _():
        send_core()
        local_sk.wait()
        local.wait()
        compress(True)

    if depth > 2:
        @pl.when((p > 0) & (p < last))
        def _():
            receive_sketch(0)
            receive_sketch(1)
            make_sketch(False)
            send_sketch()
            pl.semaphore_wait(go_sem, 1)
            send_core()
            for k in range(CHUNKS):
                core_copy(k).wait_recv()
            for k in range(CHUNKS):
                core_copy(k).wait_send()
            pass_turn()
            finish_sketch()
            carry = carry_of_previous()
            for i in range(modes):
                c_own[:, i, :] = dot(carry[:, :rank], c_own[:, i, :])
                c_oth[:, i, :] = dot(carry[:, rank:], c_oth[:, i, :])
            compress(False)

    @pl.when(p == last)
    def _():
        send_sketch()
        pl.semaphore_wait(go_sem, 1)
        send_core()
        carry = carry_of_previous()
        finish_sketch()
        top = jnp.concatenate([c_own[:, i, :] for i in range(modes)], axis=1)
        moved = dot(carry[:, :rank], top)
        for k in range(CHUNKS):
            core_copy(k).wait_recv()
        bottom = jnp.concatenate([c_oth[:, i, :] for i in range(modes)], axis=1)
        moved = moved + dot(carry[:, rank:], bottom)
        for i in range(modes):
            out_ref[:, i, :] = moved[:, i * rank : (i + 1) * rank]
        for k in range(CHUNKS):
            core_copy(k).wait_send()


def body(n_pair, depth, n_split, summand_cores, sketch_cores):
    own_core, sketch_core = summand_cores[0, 0], sketch_cores[0]
    rank, modes, _ = own_core.shape
    scale = (rank * modes * n_split) ** 0.5
    square, wide = (rank, rank), (rank, 2 * rank)
    others = n_split - 1
    vmem = lambda *shape: pltpu.VMEM(shape, jnp.float32)
    sems = lambda *shape: pltpu.SemaphoreType.DMA(shape)
    out = pl.pallas_call(
        functools.partial(kernel, n_pair, depth, n_split, n_pair // 4),
        out_shape=jax.ShapeDtypeStruct(own_core.shape, jnp.float32),
        in_specs=[pl.BlockSpec(memory_space=pltpu.HBM)] * 2,
        out_specs=pl.BlockSpec(memory_space=pltpu.VMEM),
        scratch_shapes=[
            vmem(*own_core.shape), vmem(*own_core.shape),
            pltpu.VMEM(sketch_core.shape, sketch_core.dtype), vmem(*sketch_core.shape), vmem(*own_core.shape),
            vmem(*square), vmem(2, n_split, *square),
            vmem(*square), vmem(others, *square), vmem(n_split, *square),
            vmem(*wide), vmem(n_split, *wide),
            vmem(*square),
            pltpu.SemaphoreType.DMA, pltpu.SemaphoreType.DMA,
            sems(CHUNKS), sems(CHUNKS),
            sems(2, n_split), sems(2, n_split),
            sems(others), sems(others),
            sems(n_split), sems(n_split),
            sems(n_split), sems(n_split),
            pltpu.SemaphoreType.REGULAR,
        ],
        compiler_params=pltpu.CompilerParams(
            collective_id=0, has_side_effects=True, vmem_limit_bytes=65000 * 1024
        ),
    )(own_core, sketch_core)
    return (out * scale)[None, None]


def solution(mesh):
    in_specs = (P("pair", "cores", None, "split", None), P("cores", None, "split", None))
    out_specs = P("pair", "cores", None, "split", None)
    inner = functools.partial(body, mesh.shape["pair"], mesh.shape["cores"], mesh.shape["split"])
    return jax.shard_map(inner, mesh=mesh, in_specs=in_specs, out_specs=out_specs, check_vma=False)
```
